512 devices in a mesh: narrow: 8 (over z_hi, core), wide: 64 (over x, y, z_lo).
Axes of the slice: x: 4, y: 8, z: 8 (z_hi: 4, z_lo: 2; z = z_hi * 2 + z_lo), core: 2. Of those that a mesh axis runs over, the one named last changes fastest.
Arguments:
- images: float32 [65536, 1024], P(('narrow', 'wide')), may hold values from -0.25 to 0.25
- texts: float32 [65536, 1024], P(('narrow', 'wide')), may hold values from -0.25 to 0.25
- lang_ids: int32 [65536], P(('narrow', 'wide')), may hold values from 0 to 108
- lang_table: int32 [109], replicated, may hold values from 1 to 16
- log_scale: float32 [1], replicated, may hold values from 1.5 to 2.5
- bias: float32 [1], replicated, may hold values from -3.5 to -1.5
Outputs:
- grad_images: float32 [65536, 1024], P(('narrow', 'wide'))
- grad_texts: float32 [65536, 1024], P(('narrow', 'wide'))
The draws below stay inside these ranges and needn't reach their ends.
Inputs may be any that keep to these rules, and one draw needn't show every extreme that they name: lang_ids index lang_table.
All inputs are finite; a program needn't handle non-finite values.
Results may differ from the reference program's by a relative error of at most 0.00011.
Values sent between devices are 32-bit elements; how exact they have to be, the bound alone decides.
A program may use at most 64 MiB of HBM per device.

```python
import math
import jax
import jax.numpy as jnp
import numpy as np
from jax import lax

D = 1024
LANGS = 109
ROWS_DEV = 128
OFFSETS = 4
STRIDE = 8
BATCH = 65536
N_NARROW = 8
N_WIDE = 64


def set_ends(result, key, least, largest):
    shape = result.shape
    index_at = [jax.random.randint(jax.random.fold_in(key, axis), (), 0, shape[axis]) for axis in range(len(shape))]
    result = result.at[tuple(index_at)].set(least)
    longest = shape.index(max(shape))
    index_at[longest] = (index_at[longest] + 1) % shape[longest]
    return result.at[tuple(index_at)].set(largest)


def block_levels(rng, dims, cuts, smallest, high):
    level, own = 1.0, jax.random.fold_in(rng, 6)
    for position, shards_of in cuts:
        draws = jnp.exp(jax.random.uniform(jax.random.fold_in(own, position), (shards_of,), jnp.float32, smallest / len(cuts), high / len(cuts)))
        level = level * jnp.repeat(draws, dims[position] // shards_of).reshape([-1 if axis == position else 1 for axis in range(len(dims))])
    return level


def rank_bounds(count, lean):
    loads = [(1 << 20) // math.isqrt(grade ** lean) + 1 for grade in range(1, count + 1)]
    deviation = 1 + sum(loads) // (1 << 30)
    return np.cumsum(np.array([max(1, weight // deviation) for weight in loads]))


def ranked_ids(stream_key, shape, number_of, slope):
    table = rank_bounds(number_of, slope)
    ticket = jax.random.randint(jax.random.fold_in(stream_key, 1), shape, 0, int(table[number_of - 1]))
    standing = jnp.searchsorted(jnp.asarray(table, jnp.int32), ticket, side="right")
    return jax.random.permutation(jax.random.fold_in(stream_key, 2), number_of)[standing].astype(jnp.int32)


def centred(rng, extent, scale, bound, split=(), kind=jnp.bfloat16):
    loudness = block_levels(rng, extent, split, -0.22, 0.18) if split else 1.0
    values = jax.random.normal(rng, extent, jnp.float32) * scale * loudness
    return jnp.minimum(jnp.maximum(values, -bound), bound).astype(kind)


def setup_inputs(seed: int = 0) -> dict:
    streams_of = jax.random.split(jax.random.key(seed), 7)
    images = centred(streams_of[0], (BATCH, D), 0.03125, 0.25, ((0, 512),), jnp.float32)
    texts = centred(streams_of[1], (BATCH, D), 0.03125, 0.25, ((0, 512),), jnp.float32)
    lang_ids = set_ends(ranked_ids(streams_of[2], (BATCH,), LANGS, 2), jax.random.fold_in(streams_of[2], 3), 0, LANGS - 1).astype(jnp.int32)
    lang_table = set_ends(jax.random.randint(streams_of[3], (LANGS,), 1, 17), jax.random.fold_in(streams_of[3], 1), 1, 16).astype(jnp.int32)
    log_scale = jnp.clip(jax.random.uniform(streams_of[4], (1,), jnp.float32, 1.5, 2.5), 1.5, 2.5)
    bias = jnp.clip(jax.random.uniform(streams_of[5], (1,), jnp.float32, -3.5, -1.5), -3.5, -1.5)
    return dict(images=images, texts=texts, lang_ids=lang_ids, lang_table=lang_table, log_scale=log_scale, bias=bias)


def normalize(vectors):
    inverse = lax.rsqrt(lax.optimization_barrier(jnp.sum(vectors * vectors, axis=-1, keepdims=True)) + 1e-06)
    return (vectors * inverse, inverse)

def to_groups(array):
    shaped = array.reshape((N_NARROW, N_WIDE, ROWS_DEV) + array.shape[1:])
    moved = jnp.swapaxes(shaped, 0, 1)
    return moved.reshape((N_WIDE, N_NARROW * ROWS_DEV) + array.shape[1:])

def from_groups(array):
    shaped = array.reshape((N_WIDE, N_NARROW, ROWS_DEV) + array.shape[2:])
    moved = jnp.swapaxes(shaped, 0, 1)
    return moved.reshape((BATCH,) + array.shape[2:])

def project_back(hat_grad, unit, inverse):
    return inverse * (hat_grad - unit * lax.optimization_barrier(jnp.sum(unit * hat_grad, axis=-1, keepdims=True)))

def reference(images, texts, lang_ids, lang_table, log_scale, bias):
    img_hat, inv_img = normalize(images)
    txt_hat, inv_txt = normalize(texts)
    one_hot = lang_ids[:, None] == jnp.arange(LANGS, dtype=jnp.int32)[None, :]
    table_float = lang_table.astype(jnp.float32)
    pair_weight = lax.optimization_barrier(jnp.sum(jnp.where(one_hot, table_float[None, :], jnp.float32(0.0)), axis=1)) / 8.0
    logit_scale = jnp.exp(log_scale[0])
    logit_bias = bias[0]
    image_groups = to_groups(img_hat)
    text_groups = to_groups(txt_hat)
    weight_groups = to_groups(pair_weight)
    width = N_NARROW * ROWS_DEV
    diagonal = jnp.arange(width, dtype=jnp.int32)[:, None] == jnp.arange(width, dtype=jnp.int32)[None, :]
    image_grad = jnp.zeros(image_groups.shape, jnp.float32)
    text_grad = jnp.zeros(text_groups.shape, jnp.float32)
    hi = lax.Precision.HIGHEST
    for offset in range(OFFSETS):
        text_now = jnp.roll(text_groups, offset * STRIDE, axis=0)
        weight_now = jnp.roll(weight_groups, offset * STRIDE, axis=0)
        logits = logit_scale * jnp.einsum('gid,gjd->gij', image_groups, text_now, precision=hi) + logit_bias
        if offset == 0:
            label_sign = jnp.where(diagonal, jnp.float32(1.0), jnp.float32(-1.0))[None]
        else:
            label_sign = jnp.float32(-1.0)
        pair_grad = -(logit_scale * weight_now[:, None, :]) * label_sign * jax.nn.sigmoid(-label_sign * logits)
        image_grad = image_grad + jnp.einsum('gij,gjd->gid', pair_grad, text_now, precision=hi)
        text_part = jnp.einsum('gij,gid->gjd', pair_grad, image_groups, precision=hi)
        text_grad = text_grad + jnp.roll(text_part, -offset * STRIDE, axis=0)
    grad_images = project_back(from_groups(image_grad), img_hat, inv_img)
    grad_texts = project_back(from_groups(text_grad), txt_hat, inv_txt)
    return (grad_images, grad_texts)
```

```python
import jax
import jax.numpy as jnp
from jax import lax
from jax.experimental import pallas as pl
from jax.experimental.pallas import tpu as pltpu
from jax.sharding import PartitionSpec as P

MESH = pl.DeviceIdType.MESH
OFFSETS = 4
ROWS = 128
HALF = 64
DIM = 1024
PAIR = 2 * ROWS
NARROW = 8
WIDE = 64
PREV, NEXT, OWN, OPP = 0, 1, 2, 3
QUARTER = 32
COPIES = tuple(
    ["ia", "ib", "ja", "jb", "fa", "fb", "t1a", "t1b", "t2", "t3a", "t3b", "u2"]
    + ["w1", "w2", "w3", "ha", "hb", "sa", "sb", "dn0", "dn1", "dp0", "dp1"]
    + [f"{name}{i}" for name in ("u3", "v1", "sw", "s", "q") for i in range(4)]
)


def split(value):
    high = value.astype(jnp.bfloat16)
    low = (value - high.astype(jnp.float32)).astype(jnp.bfloat16)
    return high, low


def dot3(left, right, left_dim, right_dim):
    dims = (((left_dim,), (right_dim,)), ((), ()))

    def one(a, b):
        return lax.dot_general(a, b, dims, preferred_element_type=jnp.float32)

    return one(left[0], right[0]) + (one(left[1], right[0]) + one(left[0], right[1]))


def kernel(
    img_hbm, txt_hbm, ids_hbm, table_hbm, scale_hbm, bias_hbm, img_sum, txt_sum,
    raw, ids_ref, table_ref, scale_ref, bias_ref, load_sem, img, txt, wts, img_h, img_l, txt_h, txt_l, g_h, g_l, img_part, txt_part,
    half_a, half_b, from_prev, from_next, sib_part, got3, got1, got2, send_sem, recv_sem,
):
    n = lax.axis_index("narrow")
    w = lax.axis_index("wide")
    nxt = (lax.rem(n + 2, NARROW), w)
    prv = (lax.rem(n + NARROW - 2, NARROW), w)
    sib = (n + 1 - 2 * lax.rem(n, 2), w)
    hop = WIDE // 8
    step1, back1 = (n, lax.rem(w + hop, WIDE)), (n, lax.rem(w + WIDE - hop, WIDE))
    step2, back2 = (n, lax.rem(w + 2 * hop, WIDE)), (n, lax.rem(w + WIDE - 2 * hop, WIDE))

    barrier = pltpu.get_barrier_semaphore()
    partners = (nxt, prv, sib, step1, back1, step2, back2)
    for partner in partners:
        pl.semaphore_signal(barrier, inc=1, device_id=partner, device_id_type=MESH)

    A, B = pl.ds(0, HALF), pl.ds(HALF, HALF)
    part = [pl.ds(i * QUARTER, QUARTER) for i in range(4)]
    plan = {
        "ia": (img.at[OWN, A], img.at[PREV, A], nxt),
        "ib": (img.at[OWN, B], img.at[PREV, B], nxt),
        "ja": (img.at[OWN, A], img.at[NEXT, A], prv),
        "jb": (img.at[OWN, B], img.at[NEXT, B], prv),
        "fa": (img.at[PREV, A], img.at[OPP, A], nxt),
        "fb": (img.at[NEXT, B], img.at[OPP, B], prv),
        "ha": (img_part.at[OPP, A], half_a, nxt),
        "hb": (img_part.at[OPP, B], half_b, prv),
        "sa": (img_part.at[NEXT, A], from_prev.at[A], nxt),
        "sb": (img_part.at[PREV, B], from_next.at[B], prv),
        "t1a": (txt.at[0, 0, A], txt.at[1, 0, A], step1),
        "t1b": (txt.at[0, 0, B], txt.at[1, 0, B], step1),
        "t3a": (txt.at[1, 0, A], txt.at[3, 0, A], step2),
        "t3b": (txt.at[1, 0, B], txt.at[3, 0, B], step2),
        "t2": (txt.at[0, 0], txt.at[2, 0], step2),
        "u2": (txt_part.at[2, 0], got2, back2),
        "w1": (wts.at[0, 0], wts.at[1, 0], step1),
        "w2": (wts.at[0, 0], wts.at[2, 0], step2),
        "w3": (wts.at[1, 0], wts.at[3, 0], step2),
    }
    for i in range(4):
        plan[f"u3{i}"] = (txt_part.at[3, 0, part[i]], got3.at[part[i]], back2)
        plan[f"v1{i}"] = (txt_part.at[1, 0, part[i]], got1.at[part[i]], back1)
        plan[f"sw{i}"] = (wts.at[i, 0], wts.at[i, 1], sib)
        plan[f"s{i}"] = (txt.at[i, 0], txt.at[i, 1], sib)
        plan[f"q{i}"] = (txt_part.at[i, 1], sib_part.at[i], sib)
    for i in range(2):
        low, high = part[i], part[2 + i]
        plan[f"dn{i}"] = (img_part.at[NEXT, high], from_prev.at[high], nxt)
        plan[f"dp{i}"] = (img_part.at[PREV, low], from_next.at[low], prv)

    def copy(name):
        src, dst, device = plan[name]
        i = COPIES.index(name)
        return pltpu.make_async_remote_copy(
            src_ref=src, dst_ref=dst, send_sem=send_sem.at[i], recv_sem=recv_sem.at[i],
            device_id=device, device_id_type=MESH,
        )

    def start(*names):
        for name in names:
            copy(name).start()

    done = set()

    def sent(*names):
        for name in names:
            copy(name).wait_send()
            done.add(name)

    def arrived(*names):
        for name in names:
            copy(name).wait_recv()

    loads = [
        pltpu.make_async_copy(src, dst, load_sem.at[i])
        for i, (src, dst) in enumerate(
            [(img_hbm, raw.at[0]), (txt_hbm, raw.at[1]), (ids_hbm, ids_ref),
             (table_hbm, table_ref), (scale_hbm, scale_ref), (bias_hbm, bias_ref)]
        )
    ]
    for load in loads:
        load.start()

    def unit_rows(which):
        rows = raw[which]
        return rows * lax.rsqrt(jnp.sum(rows * rows, axis=-1, keepdims=True) + 1e-06)

    loads[0].wait()
    img[OWN] = unit_rows(0)
    pl.semaphore_wait(barrier, len(partners))
    start("ia", "jb", "ib", "ja")
    loads[1].wait()
    txt[0, 0] = unit_rows(1)
    start("t1a", "t1b", "t2", "s0")
    for load in loads[2:]:
        load.wait()
    ids = jnp.broadcast_to(ids_ref[...], (8, ROWS))
    weight = jnp.zeros((8, ROWS), jnp.int32)
    for language in range(table_ref.shape[0]):
        weight = jnp.where(ids == language, table_ref[language], weight)
    wts[0, 0] = weight.astype(jnp.float32) / 8.0
    start("w1", "w2", "sw0")

    logit_scale = jnp.exp(jnp.full((1, ROWS), scale_ref[0], jnp.float32))[:, :1]
    logit_bias = bias_ref[0]

    def split_image(slot):
        rows = pl.ds(slot * ROWS, ROWS)
        img_h[rows, :], img_l[rows, :] = split(img[slot])

    def split_text(k, side):
        rows = pl.ds(k * PAIR + side * ROWS, ROWS)
        txt_h[rows, :], txt_l[rows, :] = split(txt[k, side])

    def pair_grads(first, count, k):
        rows, cols = pl.ds(first * ROWS, count * ROWS), pl.ds(k * PAIR, PAIR)
        dots = dot3((img_h[rows, :], img_l[rows, :]), (txt_h[cols, :], txt_l[cols, :]), 1, 1)
        logits = logit_scale * dots + logit_bias
        pair_w = jnp.concatenate([wts[k, 0, 0:1, :], wts[k, 1, 0:1, :]], axis=1)
        factor = jnp.broadcast_to(logit_scale * pair_w, logits.shape)
        if k == 0 and first <= OWN < first + count:
            row = lax.broadcasted_iota(jnp.int32, logits.shape, 0) - (OWN - first) * ROWS
            positive = row == lax.broadcasted_iota(jnp.int32, logits.shape, 1)
            logits = jnp.where(positive, -logits, logits)
            factor = jnp.where(positive, -factor, factor)
        grads = factor / (1.0 + jnp.exp(-logits))
        g_h[rows, cols], g_l[rows, cols] = split(grads)

    def image_grads(first, count):
        rows = pl.ds(first * ROWS, count * ROWS)
        for tile in range(DIM // PAIR):
            cols = pl.ds(tile * PAIR, PAIR)
            part = dot3((g_h[rows, :], g_l[rows, :]), (txt_h[:, cols], txt_l[:, cols]), 1, 0)
            for slot in range(count):
                img_part[first + slot, :, cols] = part[slot * ROWS:(slot + 1) * ROWS]

    def text_grads(k):
        rows = pl.ds(k * PAIR, PAIR)
        for tile in range(DIM // PAIR):
            cols = pl.ds(tile * PAIR, PAIR)
            part = dot3((g_h[:, rows], g_l[:, rows]), (img_h[:, cols], img_l[:, cols]), 0, 0)
            txt_part[k, 0, :, cols] = part[:ROWS]
            txt_part[k, 1, :, cols] = part[ROWS:]

    split_image(OWN)
    split_text(0, 0)
    arrived("s0", "sw0")
    split_text(0, 1)

    arrived("ia")
    start("fa")
    arrived("jb")
    start("fb")
    arrived("t1a")
    start("t3a")
    arrived("t2")
    start("s2")
    arrived("w1", "w2")
    start("w3", "sw1", "sw2")
    arrived("t1b")
    start("t3b", "s1")
    arrived("ib")
    split_image(PREV)
    arrived("ja")
    split_image(NEXT)
    split_text(1, 0)
    split_text(2, 0)
    pair_grads(PREV, 3, 0)
    arrived("s2", "sw2")
    split_text(2, 1)
    pair_grads(PREV, 3, 2)
    arrived("s1", "sw1")
    split_text(1, 1)
    pair_grads(PREV, 3, 1)
    arrived("w3")
    start("sw3")
    arrived("t3a", "t3b")
    start("s3")
    split_text(3, 0)
    arrived("s3", "sw3")
    split_text(3, 1)
    pair_grads(PREV, 3, 3)
    image_grads(PREV, 2)
    start("dn0", "dp0")

    arrived("fa", "fb")
    split_image(OPP)
    pair_grads(OPP, 1, 3)
    text_grads(3)
    start("q3")
    pair_grads(OPP, 1, 1)
    pair_grads(OPP, 1, 0)
    arrived("q3")
    txt_part[3, 0] += sib_part[3]
    start("u30")
    pair_grads(OPP, 1, 2)
    image_grads(OPP, 1)
    start("ha", "hb")
    text_grads(1)
    start("q1")
    sent("u30")
    start("u31")
    text_grads(2)
    start("q2")
    arrived("q1")
    txt_part[1, 0] += sib_part[1]
    for i in range(4):
        arrived(f"u3{i}")
        txt_part[1, 0, part[i]] += got3[part[i]]
        start(f"v1{i}")
        if i < 2:
            sent(f"u3{i + 1}")
            start(f"u3{i + 2}")
        if i == 0:
            text_grads(0)
            start("q0")
        if i == 1:
            image_grads(OWN, 1)
    arrived("q2")
    txt_part[2, 0] += sib_part[2]
    sent("u33")
    start("u2")
    sent("ha", "hb")
    start("dn1", "dp1")
    arrived("ha")
    img_part[NEXT, A] += half_a[...]
    start("sa")
    arrived("hb")
    img_part[PREV, B] += half_b[...]
    start("sb")
    arrived("q0")
    txt_part[0, 0] += sib_part[0]

    arrived("dn0", "dn1", "dp0", "dp1", "sa", "sb")
    img_sum[...] = img_part[OWN] + from_prev[...] + from_next[...]
    arrived("u2", "v10", "v11", "v12", "v13")
    txt_sum[...] = txt_part[0, 0] + got1[...] + got2[...]
    for name in COPIES:
        if name not in done:
            copy(name).wait_send()


def project_back(img_ref, txt_ref, img_sum, txt_sum, gimg_ref, gtxt_ref):
    for rows, total, out in ((img_ref, img_sum, gimg_ref), (txt_ref, txt_sum, gtxt_ref)):
        vectors = rows[...]
        inverse = lax.rsqrt(jnp.sum(vectors * vectors, axis=-1, keepdims=True) + 1e-06)
        unit = vectors * inverse
        hat_grad = total[...]
        along = jnp.sum(unit * hat_grad, axis=-1, keepdims=True)
        out[...] = inverse * (hat_grad - unit * along)


def on_device(images, texts, lang_ids, lang_table, log_scale, bias):
    vmem = pl.BlockSpec(memory_space=pltpu.VMEM)
    anywhere = pl.BlockSpec(memory_space=pl.ANY)
    f32, bf16 = jnp.float32, jnp.bfloat16
    block = (ROWS, DIM)
    half = (HALF, DIM)
    out = jax.ShapeDtypeStruct(block, f32)
    img_sum, txt_sum = pl.pallas_call(
        kernel,
        out_shape=(out, out),
        in_specs=[anywhere] * 6,
        out_specs=(vmem, vmem),
        scratch_shapes=[
            pltpu.VMEM((2,) + block, f32),
            pltpu.VMEM((1, ROWS), jnp.int32),
            pltpu.SMEM(lang_table.shape, jnp.int32),
            pltpu.SMEM((1,), f32),
            pltpu.SMEM((1,), f32),
            pltpu.SemaphoreType.DMA((6,)),
            pltpu.VMEM((4,) + block, f32),
            pltpu.VMEM((4, 2) + block, f32),
            pltpu.VMEM((4, 2, 8, ROWS), f32),
            pltpu.VMEM((4 * ROWS, DIM), bf16),
            pltpu.VMEM((4 * ROWS, DIM), bf16),
            pltpu.VMEM((4 * PAIR, DIM), bf16),
            pltpu.VMEM((4 * PAIR, DIM), bf16),
            pltpu.VMEM((4 * ROWS, 4 * PAIR), bf16),
            pltpu.VMEM((4 * ROWS, 4 * PAIR), bf16),
            pltpu.VMEM((4,) + block, f32),
            pltpu.VMEM((4, 2) + block, f32),
            pltpu.VMEM(half, f32),
            pltpu.VMEM(half, f32),
            pltpu.VMEM(block, f32),
            pltpu.VMEM(block, f32),
            pltpu.VMEM((4,) + block, f32),
            pltpu.VMEM(block, f32),
            pltpu.VMEM(block, f32),
            pltpu.VMEM(block, f32),
            pltpu.SemaphoreType.DMA((len(COPIES),)),
            pltpu.SemaphoreType.DMA((len(COPIES),)),
        ],
        compiler_params=pltpu.CompilerParams(
            collective_id=0, has_side_effects=True, vmem_limit_bytes=56 * 2**20
        ),
        cost_estimate=pl.CostEstimate(
            flops=9 * 2 * 512 * 1024 * 1024, bytes_accessed=4 * 2**19, transcendentals=2**19
        ),
    )(images, texts, lang_ids.reshape(1, ROWS), lang_table, log_scale, bias)
    return pl.pallas_call(
        project_back,
        out_shape=(out, out),
        in_specs=[vmem] * 4,
        out_specs=(vmem, vmem),
        cost_estimate=pl.CostEstimate(flops=2**20, bytes_accessed=6 * 2**19, transcendentals=256),
    )(images, texts, img_sum, txt_sum)


def solution(mesh):
    placed = (
        P(("narrow", "wide"), None),
        P(("narrow", "wide"), None),
        P(("narrow", "wide")),
        P(),
        P(),
        P(),
    )
    return jax.shard_map(
        on_device,
        mesh=mesh,
        in_specs=placed,
        out_specs=(P(("narrow", "wide"), None), P(("narrow", "wide"), None)),
        check_vma=False,
    )
```

```python
import jax
import jax.numpy as jnp
from jax import lax
from jax.experimental import pallas as pl
from jax.experimental.pallas import tpu as pltpu
from jax.sharding import PartitionSpec as P

MESH = pl.DeviceIdType.MESH
OFFSETS = 4
ROWS = 128
HALF = 64
DIM = 1024
PAIR = 2 * ROWS
NARROW = 8
WIDE = 64
PREV, NEXT, OWN, OPP = 0, 1, 2, 3
QUARTER = 32
COPIES = tuple(
    ["ia", "ib", "ja", "jb", "fa", "fb", "t1a", "t1b", "t2", "t3a", "t3b", "s3a", "s3b"]
    + ["w1", "w2", "w3", "ha", "hb", "sa", "sb", "dn0", "dn1", "dp0", "dp1"]
    + [f"{name}{i}" for name in ("u3", "v1", "u2", "sw", "q") for i in range(4)]
    + ["s0", "s1", "s2"]
)


def split(value):
    high = value.astype(jnp.bfloat16)
    low = (value - high.astype(jnp.float32)).astype(jnp.bfloat16)
    return high, low


def dot3(left, right, left_dim, right_dim):
    dims = (((left_dim,), (right_dim,)), ((), ()))

    def one(a, b):
        return lax.dot_general(a, b, dims, preferred_element_type=jnp.float32)

    return one(left[0], right[0]) + (one(left[1], right[0]) + one(left[0], right[1]))


def kernel(
    img_hbm, txt_hbm, ids_hbm, table_hbm, scale_hbm, bias_hbm, img_sum, txt_sum,
    raw, ids_ref, table_ref, scale_ref, bias_ref, load_sem, img, txt, wts, img_h, img_l, txt_h, txt_l, g_h, g_l, img_part, txt_part,
    half_a, half_b, from_prev, from_next, sib_part, got3, got1, got2, send_sem, recv_sem,
):
    n = lax.axis_index("narrow")
    w = lax.axis_index("wide")
    nxt = (lax.rem(n + 2, NARROW), w)
    prv = (lax.rem(n + NARROW - 2, NARROW), w)
    sib = (n + 1 - 2 * lax.rem(n, 2), w)
    hop = WIDE // 8
    odd = lax.rem(w // hop, 2)
    across = (n, w + hop - 2 * hop * odd)
    step1, back1 = (n, lax.rem(w + hop, WIDE)), (n, lax.rem(w + WIDE - hop, WIDE))
    step2, back2 = (n, lax.rem(w + 2 * hop, WIDE)), (n, lax.rem(w + WIDE - 2 * hop, WIDE))

    barrier = pltpu.get_barrier_semaphore()
    partners = (nxt, prv, sib, step1, back1, step2, back2)
    for partner in partners:
        pl.semaphore_signal(barrier, inc=1, device_id=partner, device_id_type=MESH)

    A, B = pl.ds(0, HALF), pl.ds(HALF, HALF)
    part = [pl.ds(i * QUARTER, QUARTER) for i in range(4)]
    plan = {
        "ia": (img.at[OWN, A], img.at[PREV, A], nxt),
        "ib": (img.at[OWN, B], img.at[PREV, B], nxt),
        "ja": (img.at[OWN, A], img.at[NEXT, A], prv),
        "jb": (img.at[OWN, B], img.at[NEXT, B], prv),
        "fa": (img.at[PREV, A], img.at[OPP, A], nxt),
        "fb": (img.at[NEXT, B], img.at[OPP, B], prv),
        "ha": (img_part.at[OPP, A], half_a, nxt),
        "hb": (img_part.at[OPP, B], half_b, prv),
        "sa": (img_part.at[NEXT, A], from_prev.at[A], nxt),
        "sb": (img_part.at[PREV, B], from_next.at[B], prv),
        "t1a": (txt.at[0, 0, A], txt.at[1, 0, A], step1),
        "t1b": (txt.at[0, 0, B], txt.at[1, 0, B], step1),
        "t3a": (txt.at[1, 0, A], txt.at[3, 0, A], step2),
        "t3b": (txt.at[1, 0, B], txt.at[3, 0, B], step2),
        "s3a": (txt.at[3, 0, A], txt.at[3, 1, A], sib),
        "s3b": (txt.at[3, 0, B], txt.at[3, 1, B], sib),
        "t2": (txt.at[0, 0], txt.at[2, 0], step2),
        "w1": (wts.at[0, 0], wts.at[1, 0], step1),
        "w2": (wts.at[0, 0], wts.at[2, 0], step2),
        "w3": (wts.at[1, 0], wts.at[3, 0], step2),
    }
    for i in range(4):
        plan[f"u3{i}"] = (txt_part.at[3, 0, part[i]], got3.at[part[i]], back2)
        plan[f"v1{i}"] = (txt_part.at[1, 0, part[i]], got1.at[part[i]], across)
        plan[f"u2{i}"] = (txt_part.at[2, 0, part[i]], got2.at[part[i]], back2)
        plan[f"sw{i}"] = (wts.at[i, 0], wts.at[i, 1], sib)
        plan[f"q{i}"] = (txt_part.at[i, 1], sib_part.at[i], sib)
    for i in range(3):
        plan[f"s{i}"] = (txt.at[i, 0], txt.at[i, 1], sib)
    for i in range(2):
        low, high = part[i], part[2 + i]
        plan[f"dn{i}"] = (img_part.at[NEXT, high], from_prev.at[high], nxt)
        plan[f"dp{i}"] = (img_part.at[PREV, low], from_next.at[low], prv)

    def copy(name):
        src, dst, device = plan[name]
        i = COPIES.index(name)
        return pltpu.make_async_remote_copy(
            src_ref=src, dst_ref=dst, send_sem=send_sem.at[i], recv_sem=recv_sem.at[i],
            device_id=device, device_id_type=MESH,
        )

    def start(*names):
        for name in names:
            copy(name).start()

    done = set()

    def sent(*names):
        for name in names:
            copy(name).wait_send()
            done.add(name)

    def arrived(*names):
        for name in names:
            copy(name).wait_recv()

    loads = [
        pltpu.make_async_copy(src, dst, load_sem.at[i])
        for i, (src, dst) in enumerate(
            [(img_hbm, raw.at[0]), (txt_hbm, raw.at[1]), (ids_hbm, ids_ref),
             (table_hbm, table_ref), (scale_hbm, scale_ref), (bias_hbm, bias_ref)]
        )
    ]
    for load in loads:
        load.start()

    def unit_rows(which):
        rows = raw[which]
        return rows * lax.rsqrt(jnp.sum(rows * rows, axis=-1, keepdims=True) + 1e-06)

    loads[0].wait()
    img[OWN] = unit_rows(0)
    pl.semaphore_wait(barrier, len(partners))
    start("ia", "jb", "ib", "ja")
    loads[1].wait()
    txt[0, 0] = unit_rows(1)
    start("t1a", "t1b", "t2", "s0")
    for load in loads[2:]:
        load.wait()
    ids = jnp.broadcast_to(ids_ref[...], (8, ROWS))
    weight = jnp.zeros((8, ROWS), jnp.int32)
    for language in range(table_ref.shape[0]):
        weight = jnp.where(ids == language, table_ref[language], weight)
    wts[0, 0] = weight.astype(jnp.float32) / 8.0
    start("w1", "w2", "sw0")

    logit_scale = jnp.exp(jnp.full((1, ROWS), scale_ref[0], jnp.float32))[:, :1]
    logit_bias = bias_ref[0]

    def split_image(slot):
        rows = pl.ds(slot * ROWS, ROWS)
        img_h[rows, :], img_l[rows, :] = split(img[slot])

    def split_text(k, side):
        rows = pl.ds(k * PAIR + side * ROWS, ROWS)
        txt_h[rows, :], txt_l[rows, :] = split(txt[k, side])

    def pair_grads(first, count, k):
        rows, cols = pl.ds(first * ROWS, count * ROWS), pl.ds(k * PAIR, PAIR)
        dots = dot3((img_h[rows, :], img_l[rows, :]), (txt_h[cols, :], txt_l[cols, :]), 1, 1)
        logits = logit_scale * dots + logit_bias
        pair_w = jnp.concatenate([wts[k, 0, 0:1, :], wts[k, 1, 0:1, :]], axis=1)
        factor = jnp.broadcast_to(logit_scale * pair_w, logits.shape)
        if k == 0 and first <= OWN < first + count:
            row = lax.broadcasted_iota(jnp.int32, logits.shape, 0) - (OWN - first) * ROWS
            positive = row == lax.broadcasted_iota(jnp.int32, logits.shape, 1)
            logits = jnp.where(positive, -logits, logits)
            factor = jnp.where(positive, -factor, factor)
        grads = factor / (1.0 + jnp.exp(-logits))
        g_h[rows, cols], g_l[rows, cols] = split(grads)

    def image_grads(first, count, begin=0, end=OFFSETS):
        rows, inner = pl.ds(first * ROWS, count * ROWS), pl.ds(begin * PAIR, (end - begin) * PAIR)
        for tile in range(DIM // PAIR):
            cols = pl.ds(tile * PAIR, PAIR)
            grads = dot3((g_h[rows, inner], g_l[rows, inner]), (txt_h[inner, cols], txt_l[inner, cols]), 1, 0)
            for slot in range(count):
                block = grads[slot * ROWS:(slot + 1) * ROWS]
                if begin:
                    img_part[first + slot, :, cols] += block
                else:
                    img_part[first + slot, :, cols] = block

    def text_grads(k):
        rows = pl.ds(k * PAIR, PAIR)
        for tile in range(DIM // PAIR):
            cols = pl.ds(tile * PAIR, PAIR)
            part = dot3((g_h[:, rows], g_l[:, rows]), (img_h[:, cols], img_l[:, cols]), 0, 0)
            txt_part[k, 0, :, cols] = part[:ROWS]
            txt_part[k, 1, :, cols] = part[ROWS:]

    split_image(OWN)
    split_text(0, 0)
    arrived("s0", "sw0")
    split_text(0, 1)

    arrived("ia")
    start("fa")
    arrived("jb")
    start("fb")
    arrived("t1a")
    start("t3a")
    arrived("t2")
    start("s2")
    arrived("w1", "w2")
    start("w3", "sw1", "sw2")
    arrived("t1b")
    start("t3b", "s1")
    arrived("ib")
    split_image(PREV)
    arrived("ja")
    split_image(NEXT)
    split_text(1, 0)
    split_text(2, 0)
    pair_grads(PREV, 3, 0)
    arrived("s2", "sw2")
    split_text(2, 1)
    pair_grads(PREV, 3, 2)
    arrived("s1", "sw1")
    split_text(1, 1)
    pair_grads(PREV, 3, 1)
    arrived("w3")
    start("sw3")
    image_grads(PREV, 3, 0, 3)
    arrived("t3a")
    start("s3a")
    arrived("t3b")
    start("s3b")
    split_text(3, 0)
    arrived("s3a", "s3b", "sw3")
    split_text(3, 1)
    pair_grads(PREV, 2, 3)
    image_grads(PREV, 2, 3, 4)
    start("dn0", "dp0")
    pair_grads(OWN, 1, 3)

    arrived("fa", "fb")
    split_image(OPP)
    pair_grads(OPP, 1, 3)
    text_grads(3)
    start("q3")
    pair_grads(OPP, 1, 1)
    pair_grads(OPP, 1, 0)
    arrived("q3")
    txt_part[3, 0] += sib_part[3]
    start("u30")
    pair_grads(OPP, 1, 2)
    image_grads(OPP, 1)
    start("ha", "hb")
    text_grads(1)
    start("q1")
    sent("u30")
    start("u31")
    text_grads(2)
    start("q2")
    arrived("q1")
    txt_part[1, 0] += sib_part[1]
    for i in range(4):
        arrived(f"u3{i}")
        txt_part[1, 0, part[i]] += got3[part[i]]
        start(f"v1{i}")
        if i < 2:
            sent(f"u3{i + 1}")
            start(f"u3{i + 2}")
        if i == 0:
            text_grads(0)
            start("q0")
        if i == 1:
            image_grads(OWN, 1, 3, 4)
    sent("ha", "hb")
    start("dn1", "dp1")
    arrived("ha")
    img_part[NEXT, A] += half_a[...]
    start("sa")
    arrived("hb")
    img_part[PREV, B] += half_b[...]
    start("sb")
    arrived("q2")
    txt_part[2, 0] += sib_part[2]

    @pl.when(odd == 0)
    def _():
        start("u20", "u21", "u22", "u23")

    arrived("q0")
    txt_part[0, 0] += sib_part[0]

    @pl.when(odd == 1)
    def _():
        for i in range(4):
            arrived(f"v1{i}")
            txt_part[2, 0, part[i]] += got1[part[i]]
            start(f"u2{i}")

    arrived("dn0", "dn1", "dp0", "dp1", "sa", "sb")
    img_sum[...] = img_part[OWN] + from_prev[...] + from_next[...]

    @pl.when(odd == 0)
    def _():
        arrived("v10", "v11", "v12", "v13")
        txt_part[0, 0] += got1[...]

    arrived("u20", "u21", "u22", "u23")
    txt_sum[...] = txt_part[0, 0] + got2[...]
    for name in COPIES:
        if name not in done:
            copy(name).wait_send()


def project_back(img_ref, txt_ref, img_sum, txt_sum, gimg_ref, gtxt_ref):
    for rows, total, out in ((img_ref, img_sum, gimg_ref), (txt_ref, txt_sum, gtxt_ref)):
        vectors = rows[...]
        inverse = lax.rsqrt(jnp.sum(vectors * vectors, axis=-1, keepdims=True) + 1e-06)
        unit = vectors * inverse
        hat_grad = total[...]
        along = jnp.sum(unit * hat_grad, axis=-1, keepdims=True)
        out[...] = inverse * (hat_grad - unit * along)


def on_device(images, texts, lang_ids, lang_table, log_scale, bias):
    vmem = pl.BlockSpec(memory_space=pltpu.VMEM)
    anywhere = pl.BlockSpec(memory_space=pl.ANY)
    f32, bf16 = jnp.float32, jnp.bfloat16
    block = (ROWS, DIM)
    half = (HALF, DIM)
    out = jax.ShapeDtypeStruct(block, f32)
    img_sum, txt_sum = pl.pallas_call(
        kernel,
        out_shape=(out, out),
        in_specs=[anywhere] * 6,
        out_specs=(vmem, vmem),
        scratch_shapes=[
            pltpu.VMEM((2,) + block, f32),
            pltpu.VMEM((1, ROWS), jnp.int32),
            pltpu.SMEM(lang_table.shape, jnp.int32),
            pltpu.SMEM((1,), f32),
            pltpu.SMEM((1,), f32),
            pltpu.SemaphoreType.DMA((6,)),
            pltpu.VMEM((4,) + block, f32),
            pltpu.VMEM((4, 2) + block, f32),
            pltpu.VMEM((4, 2, 8, ROWS), f32),
            pltpu.VMEM((4 * ROWS, DIM), bf16),
            pltpu.VMEM((4 * ROWS, DIM), bf16),
            pltpu.VMEM((4 * PAIR, DIM), bf16),
            pltpu.VMEM((4 * PAIR, DIM), bf16),
            pltpu.VMEM((4 * ROWS, 4 * PAIR), bf16),
            pltpu.VMEM((4 * ROWS, 4 * PAIR), bf16),
            pltpu.VMEM((4,) + block, f32),
            pltpu.VMEM((4, 2) + block, f32),
            pltpu.VMEM(half, f32),
            pltpu.VMEM(half, f32),
            pltpu.VMEM(block, f32),
            pltpu.VMEM(block, f32),
            pltpu.VMEM((4,) + block, f32),
            pltpu.VMEM(block, f32),
            pltpu.VMEM(block, f32),
            pltpu.VMEM(block, f32),
            pltpu.SemaphoreType.DMA((len(COPIES),)),
            pltpu.SemaphoreType.DMA((len(COPIES),)),
        ],
        compiler_params=pltpu.CompilerParams(
            collective_id=0, has_side_effects=True, vmem_limit_bytes=56 * 2**20
        ),
        cost_estimate=pl.CostEstimate(
            flops=9 * 2 * 512 * 1024 * 1024, bytes_accessed=4 * 2**19, transcendentals=2**19
        ),
    )(images, texts, lang_ids.reshape(1, ROWS), lang_table, log_scale, bias)
    return pl.pallas_call(
        project_back,
        out_shape=(out, out),
        in_specs=[vmem] * 4,
        out_specs=(vmem, vmem),
        cost_estimate=pl.CostEstimate(flops=2**20, bytes_accessed=6 * 2**19, transcendentals=256),
    )(images, texts, img_sum, txt_sum)


def solution(mesh):
    placed = (
        P(("narrow", "wide"), None),
        P(("narrow", "wide"), None),
        P(("narrow", "wide")),
        P(),
        P(),
        P(),
    )
    return jax.shard_map(
        on_device,
        mesh=mesh,
        in_specs=placed,
        out_specs=(P(("narrow", "wide"), None), P(("narrow", "wide"), None)),
        check_vma=False,
    )
```

```python
import jax
import jax.numpy as jnp
from jax import lax
from jax.experimental import pallas as pl
from jax.experimental.pallas import tpu as pltpu
from jax.sharding import PartitionSpec as P

MESH = pl.DeviceIdType.MESH
OFFSETS = 4
ROWS = 128
HALF = 64
DIM = 1024
PAIR = 2 * ROWS
NARROW = 8
WIDE = 64
PREV, NEXT, OWN, OPP = 0, 1, 2, 3
QUARTER = 32
COPIES = tuple(
    ["ia", "ib", "ja", "jb", "fa", "fb", "t1a", "t1b", "t2", "t3a", "t3b", "s3a", "s3b"]
    + ["w1", "w2", "w3", "ha", "hb", "sa", "sb", "dn0", "dn1", "dp0", "dp1"]
    + [f"{name}{i}" for name in ("u3", "v1", "u2", "sw", "q") for i in range(4)]
    + ["s0", "s1", "s2"]
)


def split(value):
    high = value.astype(jnp.bfloat16)
    low = (value - high.astype(jnp.float32)).astype(jnp.bfloat16)
    return high, low


def dot3(left, right, left_dim, right_dim):
    dims = (((left_dim,), (right_dim,)), ((), ()))

    def one(a, b):
        return lax.dot_general(a, b, dims, preferred_element_type=jnp.float32)

    return one(left[0], right[0]) + (one(left[1], right[0]) + one(left[0], right[1]))


def kernel(
    img_hbm, txt_hbm, ids_hbm, table_hbm, scale_hbm, bias_hbm, gimg_ref, gtxt_ref,
    raw, ids_ref, table_ref, scale_ref, bias_ref, load_sem, img, txt, wts, img_h, img_l, txt_h, txt_l, g_h, g_l, img_part, txt_part,
    half_a, half_b, from_prev, from_next, sib_part, got3, got1, got2, send_sem, recv_sem,
):
    n = lax.axis_index("narrow")
    w = lax.axis_index("wide")
    nxt = (lax.rem(n + 2, NARROW), w)
    prv = (lax.rem(n + NARROW - 2, NARROW), w)
    sib = (n + 1 - 2 * lax.rem(n, 2), w)
    hop = WIDE // 8
    odd = lax.rem(w // hop, 2)
    across = (n, w + hop - 2 * hop * odd)
    step1, back1 = (n, lax.rem(w + hop, WIDE)), (n, lax.rem(w + WIDE - hop, WIDE))
    step2, back2 = (n, lax.rem(w + 2 * hop, WIDE)), (n, lax.rem(w + WIDE - 2 * hop, WIDE))

    barrier = pltpu.get_barrier_semaphore()
    partners = (step1, back1, nxt, prv, step2, back2, sib)
    for partner in partners:
        pl.semaphore_signal(barrier, inc=1, device_id=partner, device_id_type=MESH)

    A, B = pl.ds(0, HALF), pl.ds(HALF, HALF)
    part = [pl.ds(i * QUARTER, QUARTER) for i in range(4)]
    plan = {
        "ia": (img.at[OWN, A], img.at[PREV, A], nxt),
        "ib": (img.at[OWN, B], img.at[PREV, B], nxt),
        "ja": (img.at[OWN, A], img.at[NEXT, A], prv),
        "jb": (img.at[OWN, B], img.at[NEXT, B], prv),
        "fa": (img.at[PREV, A], img.at[OPP, A], nxt),
        "fb": (img.at[NEXT, B], img.at[OPP, B], prv),
        "ha": (img_part.at[OPP, A], half_a, nxt),
        "hb": (img_part.at[OPP, B], half_b, prv),
        "sa": (img_part.at[NEXT, A], from_prev.at[A], nxt),
        "sb": (img_part.at[PREV, B], from_next.at[B], prv),
        "t1a": (txt.at[0, 0, A], txt.at[1, 0, A], step1),
        "t1b": (txt.at[0, 0, B], txt.at[1, 0, B], step1),
        "t3a": (txt.at[1, 0, A], txt.at[3, 0, A], step2),
        "t3b": (txt.at[1, 0, B], txt.at[3, 0, B], step2),
        "s3a": (txt.at[3, 0, A], txt.at[3, 1, A], sib),
        "s3b": (txt.at[3, 0, B], txt.at[3, 1, B], sib),
        "t2": (txt.at[0, 0], txt.at[2, 0], step2),
        "w1": (wts.at[0, 0], wts.at[1, 0], step1),
        "w2": (wts.at[0, 0], wts.at[2, 0], step2),
        "w3": (wts.at[1, 0], wts.at[3, 0], step2),
    }
    for i in range(4):
        plan[f"u3{i}"] = (txt_part.at[3, 0, part[i]], got3.at[part[i]], back2)
        plan[f"v1{i}"] = (txt_part.at[1, 0, part[i]], got1.at[part[i]], across)
        plan[f"u2{i}"] = (txt_part.at[2, 0, part[i]], got2.at[part[i]], back2)
        plan[f"sw{i}"] = (wts.at[i, 0], wts.at[i, 1], sib)
        plan[f"q{i}"] = (txt_part.at[i, 1], sib_part.at[i], sib)
    for i in range(3):
        plan[f"s{i}"] = (txt.at[i, 0], txt.at[i, 1], sib)
    for i in range(2):
        low, high = part[i], part[2 + i]
        plan[f"dn{i}"] = (img_part.at[NEXT, high], from_prev.at[high], nxt)
        plan[f"dp{i}"] = (img_part.at[PREV, low], from_next.at[low], prv)

    def copy(name):
        src, dst, device = plan[name]
        i = COPIES.index(name)
        return pltpu.make_async_remote_copy(
            src_ref=src, dst_ref=dst, send_sem=send_sem.at[i], recv_sem=recv_sem.at[i],
            device_id=device, device_id_type=MESH,
        )

    def start(*names):
        for name in names:
            copy(name).start()

    done = set()

    def sent(*names):
        for name in names:
            copy(name).wait_send()
            done.add(name)

    def arrived(*names):
        for name in names:
            copy(name).wait_recv()

    loads = [
        pltpu.make_async_copy(src, dst, load_sem.at[i])
        for i, (src, dst) in enumerate(
            [(img_hbm, raw.at[0]), (txt_hbm, raw.at[1]), (ids_hbm, ids_ref),
             (table_hbm, table_ref), (scale_hbm, scale_ref), (bias_hbm, bias_ref)]
        )
    ]
    for load in loads:
        load.start()

    def unit_rows(which):
        rows = raw[which]
        return rows * lax.rsqrt(jnp.sum(rows * rows, axis=-1, keepdims=True) + 1e-06)

    loads[0].wait()
    img[OWN] = unit_rows(0)
    pl.semaphore_wait(barrier, len(partners))
    start("ia", "jb", "ib", "ja")
    loads[1].wait()
    txt[0, 0] = unit_rows(1)
    start("t1a", "t1b", "t2", "s0")
    for load in loads[2:]:
        load.wait()
    ids = jnp.broadcast_to(ids_ref[...], (8, ROWS))
    weight = jnp.zeros((8, ROWS), jnp.int32)
    for language in range(table_ref.shape[0]):
        weight = jnp.where(ids == language, table_ref[language], weight)
    wts[0, 0] = weight.astype(jnp.float32) / 8.0
    start("w1", "w2", "sw0")

    logit_scale = jnp.exp(jnp.full((1, ROWS), scale_ref[0], jnp.float32))[:, :1]
    logit_bias = bias_ref[0]

    def split_image(slot):
        rows = pl.ds(slot * ROWS, ROWS)
        img_h[rows, :], img_l[rows, :] = split(img[slot])

    def split_text(k, side):
        rows = pl.ds(k * PAIR + side * ROWS, ROWS)
        txt_h[rows, :], txt_l[rows, :] = split(txt[k, side])

    def pair_grads(first, count, k):
        rows, cols = pl.ds(first * ROWS, count * ROWS), pl.ds(k * PAIR, PAIR)
        dots = dot3((img_h[rows, :], img_l[rows, :]), (txt_h[cols, :], txt_l[cols, :]), 1, 1)
        logits = logit_scale * dots + logit_bias
        pair_w = jnp.concatenate([wts[k, 0, 0:1, :], wts[k, 1, 0:1, :]], axis=1)
        factor = jnp.broadcast_to(logit_scale * pair_w, logits.shape)
        if k == 0 and first <= OWN < first + count:
            row = lax.broadcasted_iota(jnp.int32, logits.shape, 0) - (OWN - first) * ROWS
            positive = row == lax.broadcasted_iota(jnp.int32, logits.shape, 1)
            logits = jnp.where(positive, -logits, logits)
            factor = jnp.where(positive, -factor, factor)
        grads = factor / (1.0 + jnp.exp(-logits))
        g_h[rows, cols], g_l[rows, cols] = split(grads)

    def image_grads(first, count, begin=0, end=OFFSETS):
        rows, inner = pl.ds(first * ROWS, count * ROWS), pl.ds(begin * PAIR, (end - begin) * PAIR)
        for tile in range(DIM // PAIR):
            cols = pl.ds(tile * PAIR, PAIR)
            grads = dot3((g_h[rows, inner], g_l[rows, inner]), (txt_h[inner, cols], txt_l[inner, cols]), 1, 0)
            for slot in range(count):
                block = grads[slot * ROWS:(slot + 1) * ROWS]
                if begin:
                    img_part[first + slot, :, cols] += block
                else:
                    img_part[first + slot, :, cols] = block

    def text_grads(k):
        rows = pl.ds(k * PAIR, PAIR)
        for tile in range(DIM // PAIR):
            cols = pl.ds(tile * PAIR, PAIR)
            part = dot3((g_h[:, rows], g_l[:, rows]), (img_h[:, cols], img_l[:, cols]), 0, 0)
            txt_part[k, 0, :, cols] = part[:ROWS]
            txt_part[k, 1, :, cols] = part[ROWS:]

    split_image(OWN)
    split_text(0, 0)
    arrived("s0", "sw0")
    split_text(0, 1)

    arrived("ia")
    start("fa")
    arrived("jb")
    start("fb")
    arrived("t1a")
    start("t3a")
    arrived("t2")
    start("s2")
    arrived("w1", "w2")
    start("w3", "sw1", "sw2")
    arrived("t1b")
    start("t3b", "s1")
    arrived("ib")
    split_image(PREV)
    arrived("ja")
    split_image(NEXT)
    split_text(1, 0)
    split_text(2, 0)
    pair_grads(PREV, 3, 0)
    arrived("s2", "sw2")
    split_text(2, 1)
    pair_grads(PREV, 3, 2)
    arrived("s1", "sw1")
    split_text(1, 1)
    pair_grads(PREV, 3, 1)
    arrived("w3")
    start("sw3")
    image_grads(PREV, 3, 0, 3)
    arrived("t3a")
    start("s3a")
    arrived("t3b")
    start("s3b")
    split_text(3, 0)
    arrived("s3a", "s3b", "sw3")
    split_text(3, 1)
    pair_grads(PREV, 2, 3)
    image_grads(PREV, 2, 3, 4)
    start("dn0", "dp0")
    pair_grads(OWN, 1, 3)

    arrived("fa", "fb")
    split_image(OPP)
    pair_grads(OPP, 1, 3)
    text_grads(3)
    start("q3")
    pair_grads(OPP, 1, 1)
    pair_grads(OPP, 1, 0)
    arrived("q3")
    txt_part[3, 0] += sib_part[3]
    start("u30")
    pair_grads(OPP, 1, 2)
    image_grads(OPP, 1)
    start("ha", "hb")
    text_grads(1)
    start("q1")
    sent("u30")
    start("u31")
    text_grads(2)
    start("q2")
    arrived("q1")
    txt_part[1, 0] += sib_part[1]
    for i in range(4):
        arrived(f"u3{i}")
        txt_part[1, 0, part[i]] += got3[part[i]]
        start(f"v1{i}")
        if i < 2:
            sent(f"u3{i + 1}")
            start(f"u3{i + 2}")
        if i == 0:
            text_grads(0)
            start("q0")
        if i == 1:
            image_grads(OWN, 1, 3, 4)
    sent("ha", "hb")
    start("dn1", "dp1")
    arrived("ha")
    img_part[NEXT, A] += half_a[...]
    start("sa")
    arrived("hb")
    img_part[PREV, B] += half_b[...]
    start("sb")
    arrived("q2")
    txt_part[2, 0] += sib_part[2]

    @pl.when(odd == 0)
    def _():
        start("u20", "u21", "u22", "u23")

    arrived("q0")
    txt_part[0, 0] += sib_part[0]

    @pl.when(odd == 1)
    def _():
        for i in range(4):
            arrived(f"v1{i}")
            txt_part[2, 0, part[i]] += got1[part[i]]
            start(f"u2{i}")

    def project_back(which, unit, hat_grad, out):
        rows = raw[which]
        inverse = lax.rsqrt(jnp.sum(rows * rows, axis=-1, keepdims=True) + 1e-06)
        out[...] = inverse * (hat_grad - unit * jnp.sum(unit * hat_grad, axis=-1, keepdims=True))

    arrived("dn0", "dn1", "dp0", "dp1", "sa", "sb")
    project_back(0, img[OWN], img_part[OWN] + from_prev[...] + from_next[...], gimg_ref)

    @pl.when(odd == 0)
    def _():
        arrived("v10", "v11", "v12", "v13")
        txt_part[0, 0] += got1[...]

    arrived("u20", "u21", "u22", "u23")
    project_back(1, txt[0, 0], txt_part[0, 0] + got2[...], gtxt_ref)
    for name in COPIES:
        if name not in done:
            copy(name).wait_send()


def copy_out(img_ref, txt_ref, gimg_ref, gtxt_ref):
    gimg_ref[...] = img_ref[...]
    gtxt_ref[...] = txt_ref[...]


def on_device(images, texts, lang_ids, lang_table, log_scale, bias):
    vmem = pl.BlockSpec(memory_space=pltpu.VMEM)
    anywhere = pl.BlockSpec(memory_space=pl.ANY)
    f32, bf16 = jnp.float32, jnp.bfloat16
    block = (ROWS, DIM)
    half = (HALF, DIM)
    out = jax.ShapeDtypeStruct(block, f32)
    grads = pl.pallas_call(
        kernel,
        out_shape=(out, out),
        in_specs=[anywhere] * 6,
        out_specs=(vmem, vmem),
        scratch_shapes=[
            pltpu.VMEM((2,) + block, f32),
            pltpu.VMEM((1, ROWS), jnp.int32),
            pltpu.SMEM(lang_table.shape, jnp.int32),
            pltpu.SMEM((1,), f32),
            pltpu.SMEM((1,), f32),
            pltpu.SemaphoreType.DMA((6,)),
            pltpu.VMEM((4,) + block, f32),
            pltpu.VMEM((4, 2) + block, f32),
            pltpu.VMEM((4, 2, 8, ROWS), f32),
            pltpu.VMEM((4 * ROWS, DIM), bf16),
            pltpu.VMEM((4 * ROWS, DIM), bf16),
            pltpu.VMEM((4 * PAIR, DIM), bf16),
            pltpu.VMEM((4 * PAIR, DIM), bf16),
            pltpu.VMEM((4 * ROWS, 4 * PAIR), bf16),
            pltpu.VMEM((4 * ROWS, 4 * PAIR), bf16),
            pltpu.VMEM((4,) + block, f32),
            pltpu.VMEM((4, 2) + block, f32),
            pltpu.VMEM(half, f32),
            pltpu.VMEM(half, f32),
            pltpu.VMEM(block, f32),
            pltpu.VMEM(block, f32),
            pltpu.VMEM((4,) + block, f32),
            pltpu.VMEM(block, f32),
            pltpu.VMEM(block, f32),
            pltpu.VMEM(block, f32),
            pltpu.SemaphoreType.DMA((len(COPIES),)),
            pltpu.SemaphoreType.DMA((len(COPIES),)),
        ],
        compiler_params=pltpu.CompilerParams(
            collective_id=0, has_side_effects=True, vmem_limit_bytes=56 * 2**20
        ),
        cost_estimate=pl.CostEstimate(
            flops=9 * 2 * 512 * 1024 * 1024, bytes_accessed=4 * 2**19, transcendentals=2**19
        ),
    )(images, texts, lang_ids.reshape(1, ROWS), lang_table, log_scale, bias)
    return pl.pallas_call(
        copy_out,
        out_shape=(out, out),
        in_specs=[vmem] * 2,
        out_specs=(vmem, vmem),
        cost_estimate=pl.CostEstimate(flops=0, bytes_accessed=4 * 2**19, transcendentals=0),
    )(*grads)


def solution(mesh):
    placed = (
        P(("narrow", "wide"), None),
        P(("narrow", "wide"), None),
        P(("narrow", "wide")),
        P(),
        P(),
        P(),
    )
    return jax.shard_map(
        on_device,
        mesh=mesh,
        in_specs=placed,
        out_specs=(P(("narrow", "wide"), None), P(("narrow", "wide"), None)),
        check_vma=False,
    )
```

```python
import jax
import jax.numpy as jnp
from jax import lax
from jax.experimental import pallas as pl
from jax.experimental.pallas import tpu as pltpu
from jax.sharding import PartitionSpec as P

MESH = pl.DeviceIdType.MESH
OFFSETS = 4
ROWS = 128
HALF = 64
DIM = 1024
PAIR = 2 * ROWS
NARROW = 8
WIDE = 64
PREV, NEXT, OWN, OPP = 0, 1, 2, 3
QUARTER = 32
COPIES = tuple(
    ["ia", "ib", "ja", "jb", "fa", "fb", "t1a", "t1b", "t2", "t3a", "t3b", "s3a", "s3b"]
    + ["w1", "w2", "w3", "ha", "hb", "sa", "sb", "dn0", "dn1", "dp0", "dp1"]
    + [f"{name}{i}" for name in ("u3", "v1", "u2", "sw", "q") for i in range(4)]
    + ["s0", "s1", "s2"]
)


def split(value):
    high = value.astype(jnp.bfloat16)
    low = (value - high.astype(jnp.float32)).astype(jnp.bfloat16)
    return high, low


def dot3(left, right, left_dim, right_dim):
    dims = (((left_dim,), (right_dim,)), ((), ()))

    def one(a, b):
        return lax.dot_general(a, b, dims, preferred_element_type=jnp.float32)

    return one(left[0], right[0]) + (one(left[1], right[0]) + one(left[0], right[1]))


def kernel(
    img_hbm, txt_hbm, ids_hbm, table_hbm, scale_hbm, bias_hbm, gimg_ref, gtxt_ref,
    raw, ids_ref, table_ref, scale_ref, bias_ref, load_sem, img, txt, wts, img_h, img_l, txt_h, txt_l, g_h, g_l, img_part, txt_part,
    half_a, half_b, from_prev, from_next, sib_part, got3, got1, got2, send_sem, recv_sem,
):
    n = lax.axis_index("narrow")
    w = lax.axis_index("wide")
    nxt = (lax.rem(n + 2, NARROW), w)
    prv = (lax.rem(n + NARROW - 2, NARROW), w)
    sib = (n + 1 - 2 * lax.rem(n, 2), w)
    hop = WIDE // 8
    odd = lax.rem(w // hop, 2)
    across = (n, w + hop - 2 * hop * odd)
    step1, back1 = (n, lax.rem(w + hop, WIDE)), (n, lax.rem(w + WIDE - hop, WIDE))
    step2, back2 = (n, lax.rem(w + 2 * hop, WIDE)), (n, lax.rem(w + WIDE - 2 * hop, WIDE))

    barrier = pltpu.get_barrier_semaphore()
    partners = (step1, back1, nxt, prv, step2, back2, sib)
    for partner in partners:
        pl.semaphore_signal(barrier, inc=1, device_id=partner, device_id_type=MESH)

    A, B = pl.ds(0, HALF), pl.ds(HALF, HALF)
    part = [pl.ds(i * QUARTER, QUARTER) for i in range(4)]
    plan = {
        "ia": (img.at[OWN, A], img.at[PREV, A], nxt),
        "ib": (img.at[OWN, B], img.at[PREV, B], nxt),
        "ja": (img.at[OWN, A], img.at[NEXT, A], prv),
        "jb": (img.at[OWN, B], img.at[NEXT, B], prv),
        "fa": (img.at[PREV, A], img.at[OPP, A], nxt),
        "fb": (img.at[NEXT, B], img.at[OPP, B], prv),
        "ha": (img_part.at[OPP, A], half_a, nxt),
        "hb": (img_part.at[OPP, B], half_b, prv),
        "sa": (img_part.at[NEXT, A], from_prev.at[A], nxt),
        "sb": (img_part.at[PREV, B], from_next.at[B], prv),
        "t1a": (txt.at[0, 0, A], txt.at[1, 0, A], step1),
        "t1b": (txt.at[0, 0, B], txt.at[1, 0, B], step1),
        "t3a": (txt.at[1, 0, A], txt.at[3, 0, A], step2),
        "t3b": (txt.at[1, 0, B], txt.at[3, 0, B], step2),
        "s3a": (txt.at[3, 0, A], txt.at[3, 1, A], sib),
        "s3b": (txt.at[3, 0, B], txt.at[3, 1, B], sib),
        "t2": (txt.at[0, 0], txt.at[2, 0], step2),
        "w1": (wts.at[0, 0], wts.at[1, 0], step1),
        "w2": (wts.at[0, 0], wts.at[2, 0], step2),
        "w3": (wts.at[1, 0], wts.at[3, 0], step2),
    }
    for i in range(4):
        plan[f"u3{i}"] = (txt_part.at[3, 0, part[i]], got3.at[part[i]], back2)
        plan[f"v1{i}"] = (txt_part.at[1, 0, part[i]], got1.at[part[i]], across)
        plan[f"u2{i}"] = (txt_part.at[2, 0, part[i]], got2.at[part[i]], back2)
        plan[f"sw{i}"] = (wts.at[i, 0], wts.at[i, 1], sib)
        plan[f"q{i}"] = (txt_part.at[i, 1], sib_part.at[i], sib)
    for i in range(3):
        plan[f"s{i}"] = (txt.at[i, 0], txt.at[i, 1], sib)
    for i in range(2):
        low, high = part[i], part[2 + i]
        plan[f"dn{i}"] = (img_part.at[NEXT, high], from_prev.at[high], nxt)
        plan[f"dp{i}"] = (img_part.at[PREV, low], from_next.at[low], prv)

    def copy(name):
        src, dst, device = plan[name]
        i = COPIES.index(name)
        return pltpu.make_async_remote_copy(
            src_ref=src, dst_ref=dst, send_sem=send_sem.at[i], recv_sem=recv_sem.at[i],
            device_id=device, device_id_type=MESH,
        )

    def start(*names):
        for name in names:
            copy(name).start()

    done = set()

    def sent(*names):
        for name in names:
            copy(name).wait_send()
            done.add(name)

    def arrived(*names):
        for name in names:
            copy(name).wait_recv()

    loads = [
        pltpu.make_async_copy(src, dst, load_sem.at[i])
        for i, (src, dst) in enumerate(
            [(img_hbm, raw.at[0]), (txt_hbm, raw.at[1]), (ids_hbm, ids_ref),
             (table_hbm, table_ref), (scale_hbm, scale_ref), (bias_hbm, bias_ref)]
        )
    ]
    for load in loads:
        load.start()

    def unit_rows(which):
        rows = raw[which]
        return rows * lax.rsqrt(jnp.sum(rows * rows, axis=-1, keepdims=True) + 1e-06)

    loads[0].wait()
    img[OWN] = unit_rows(0)
    pl.semaphore_wait(barrier, len(partners))
    start("ia", "jb", "ib", "ja")
    loads[1].wait()
    txt[0, 0] = unit_rows(1)
    start("t1a", "t1b", "t2", "s0")
    for load in loads[2:]:
        load.wait()
    ids = jnp.broadcast_to(ids_ref[...], (8, ROWS))
    weight = jnp.zeros((8, ROWS), jnp.int32)
    for language in range(table_ref.shape[0]):
        weight = jnp.where(ids == language, table_ref[language], weight)
    wts[0, 0] = weight.astype(jnp.float32) / 8.0
    start("w1", "w2", "sw0")

    logit_scale = jnp.exp(jnp.full((1, ROWS), scale_ref[0], jnp.float32))[:, :1]
    logit_bias = bias_ref[0]

    def split_image(slot):
        rows = pl.ds(slot * ROWS, ROWS)
        img_h[rows, :], img_l[rows, :] = split(img[slot])

    def split_text(k, side):
        rows = pl.ds(k * PAIR + side * ROWS, ROWS)
        txt_h[rows, :], txt_l[rows, :] = split(txt[k, side])

    def pair_grads(first, count, k):
        rows, cols = pl.ds(first * ROWS, count * ROWS), pl.ds(k * PAIR, PAIR)
        dots = dot3((img_h[rows, :], img_l[rows, :]), (txt_h[cols, :], txt_l[cols, :]), 1, 1)
        logits = logit_scale * dots + logit_bias
        pair_w = jnp.concatenate([wts[k, 0, 0:1, :], wts[k, 1, 0:1, :]], axis=1)
        factor = jnp.broadcast_to(logit_scale * pair_w, logits.shape)
        if k == 0 and first <= OWN < first + count:
            row = lax.broadcasted_iota(jnp.int32, logits.shape, 0) - (OWN - first) * ROWS
            positive = row == lax.broadcasted_iota(jnp.int32, logits.shape, 1)
            logits = jnp.where(positive, -logits, logits)
            factor = jnp.where(positive, -factor, factor)
        grads = factor / (1.0 + jnp.exp(-logits))
        g_h[rows, cols], g_l[rows, cols] = split(grads)

    def image_grads(first, count, begin=0, end=OFFSETS):
        rows, inner = pl.ds(first * ROWS, count * ROWS), pl.ds(begin * PAIR, (end - begin) * PAIR)
        for tile in range(DIM // PAIR):
            cols = pl.ds(tile * PAIR, PAIR)
            grads = dot3((g_h[rows, inner], g_l[rows, inner]), (txt_h[inner, cols], txt_l[inner, cols]), 1, 0)
            for slot in range(count):
                block = grads[slot * ROWS:(slot + 1) * ROWS]
                if begin:
                    img_part[first + slot, :, cols] += block
                else:
                    img_part[first + slot, :, cols] = block

    def text_grads(k):
        rows = pl.ds(k * PAIR, PAIR)
        for tile in range(DIM // PAIR):
            cols = pl.ds(tile * PAIR, PAIR)
            part = dot3((g_h[:, rows], g_l[:, rows]), (img_h[:, cols], img_l[:, cols]), 0, 0)
            txt_part[k, 0, :, cols] = part[:ROWS]
            txt_part[k, 1, :, cols] = part[ROWS:]

    split_image(OWN)
    split_text(0, 0)
    arrived("s0", "sw0")
    split_text(0, 1)

    arrived("ia")
    start("fa")
    arrived("jb")
    start("fb")
    arrived("t1a")
    start("t3a")
    arrived("t2")
    start("s2")
    arrived("w1", "w2")
    start("w3", "sw1", "sw2")
    arrived("t1b")
    start("t3b", "s1")
    arrived("ib")
    split_image(PREV)
    arrived("ja")
    split_image(NEXT)
    split_text(1, 0)
    split_text(2, 0)
    pair_grads(PREV, 3, 0)
    arrived("s2", "sw2")
    split_text(2, 1)
    pair_grads(PREV, 3, 2)
    arrived("s1", "sw1")
    split_text(1, 1)
    pair_grads(PREV, 3, 1)
    arrived("w3")
    start("sw3")
    image_grads(PREV, 3, 0, 3)
    arrived("t3a")
    start("s3a")
    arrived("t3b")
    start("s3b")
    split_text(3, 0)
    arrived("s3a", "s3b", "sw3")
    split_text(3, 1)
    pair_grads(PREV, 2, 3)
    image_grads(PREV, 2, 3, 4)
    start("dn0", "dp0")
    pair_grads(OWN, 1, 3)

    arrived("fa", "fb")
    split_image(OPP)
    pair_grads(OPP, 1, 3)
    text_grads(3)
    start("q3")
    pair_grads(OPP, 1, 1)
    pair_grads(OPP, 1, 0)
    arrived("q3")
    txt_part[3, 0] += sib_part[3]
    start("u30", "u31")
    pair_grads(OPP, 1, 2)
    image_grads(OPP, 1)
    start("ha", "hb")
    text_grads(1)
    start("q1")
    sent("u30")
    start("u32")
    text_grads(2)
    start("q2")
    arrived("q1")
    txt_part[1, 0] += sib_part[1]
    for i in range(4):
        arrived(f"u3{i}")
        txt_part[1, 0, part[i]] += got3[part[i]]
        start(f"v1{i}")
        if i == 0:
            sent("u31")
            start("u33")
        if i == 0:
            text_grads(0)
            start("q0")
        if i == 1:
            image_grads(OWN, 1, 3, 4)
    sent("ha", "hb")
    start("dn1", "dp1")
    arrived("ha")
    img_part[NEXT, A] += half_a[...]
    start("sa")
    arrived("hb")
    img_part[PREV, B] += half_b[...]
    start("sb")
    arrived("q2")
    txt_part[2, 0] += sib_part[2]

    @pl.when(odd == 0)
    def _():
        start("u20", "u21", "u22", "u23")

    arrived("q0")
    txt_part[0, 0] += sib_part[0]

    @pl.when(odd == 1)
    def _():
        for i in range(4):
            arrived(f"v1{i}")
            txt_part[2, 0, part[i]] += got1[part[i]]
            start(f"u2{i}")

    def project_back(which, unit, hat_grad, out):
        rows = raw[which]
        inverse = lax.rsqrt(jnp.sum(rows * rows, axis=-1, keepdims=True) + 1e-06)
        out[...] = inverse * (hat_grad - unit * jnp.sum(unit * hat_grad, axis=-1, keepdims=True))

    arrived("dn0", "dn1", "dp0", "dp1", "sa", "sb")
    project_back(0, img[OWN], img_part[OWN] + from_prev[...] + from_next[...], gimg_ref)

    @pl.when(odd == 0)
    def _():
        arrived("v10", "v11", "v12", "v13")
        txt_part[0, 0] += got1[...]

    arrived("u20", "u21", "u22", "u23")
    project_back(1, txt[0, 0], txt_part[0, 0] + got2[...], gtxt_ref)
    for name in COPIES:
        if name not in done:
            copy(name).wait_send()


def copy_out(img_ref, txt_ref, gimg_ref, gtxt_ref):
    gimg_ref[...] = img_ref[...]
    gtxt_ref[...] = txt_ref[...]


def on_device(images, texts, lang_ids, lang_table, log_scale, bias):
    vmem = pl.BlockSpec(memory_space=pltpu.VMEM)
    anywhere = pl.BlockSpec(memory_space=pl.ANY)
    f32, bf16 = jnp.float32, jnp.bfloat16
    block = (ROWS, DIM)
    half = (HALF, DIM)
    out = jax.ShapeDtypeStruct(block, f32)
    grads = pl.pallas_call(
        kernel,
        out_shape=(out, out),
        in_specs=[anywhere] * 6,
        out_specs=(vmem, vmem),
        scratch_shapes=[
            pltpu.VMEM((2,) + block, f32),
            pltpu.VMEM((1, ROWS), jnp.int32),
            pltpu.SMEM(lang_table.shape, jnp.int32),
            pltpu.SMEM((1,), f32),
            pltpu.SMEM((1,), f32),
            pltpu.SemaphoreType.DMA((6,)),
            pltpu.VMEM((4,) + block, f32),
            pltpu.VMEM((4, 2) + block, f32),
            pltpu.VMEM((4, 2, 8, ROWS), f32),
            pltpu.VMEM((4 * ROWS, DIM), bf16),
            pltpu.VMEM((4 * ROWS, DIM), bf16),
            pltpu.VMEM((4 * PAIR, DIM), bf16),
            pltpu.VMEM((4 * PAIR, DIM), bf16),
            pltpu.VMEM((4 * ROWS, 4 * PAIR), bf16),
            pltpu.VMEM((4 * ROWS, 4 * PAIR), bf16),
            pltpu.VMEM((4,) + block, f32),
            pltpu.VMEM((4, 2) + block, f32),
            pltpu.VMEM(half, f32),
            pltpu.VMEM(half, f32),
            pltpu.VMEM(block, f32),
            pltpu.VMEM(block, f32),
            pltpu.VMEM((4,) + block, f32),
            pltpu.VMEM(block, f32),
            pltpu.VMEM(block, f32),
            pltpu.VMEM(block, f32),
            pltpu.SemaphoreType.DMA((len(COPIES),)),
            pltpu.SemaphoreType.DMA((len(COPIES),)),
        ],
        compiler_params=pltpu.CompilerParams(
            collective_id=0, has_side_effects=True, vmem_limit_bytes=56 * 2**20
        ),
        cost_estimate=pl.CostEstimate(
            flops=9 * 2 * 512 * 1024 * 1024, bytes_accessed=4 * 2**19, transcendentals=2**19
        ),
    )(images, texts, lang_ids.reshape(1, ROWS), lang_table, log_scale, bias)
    return pl.pallas_call(
        copy_out,
        out_shape=(out, out),
        in_specs=[vmem] * 2,
        out_specs=(vmem, vmem),
        cost_estimate=pl.CostEstimate(flops=0, bytes_accessed=4 * 2**19, transcendentals=0),
    )(*grads)


def solution(mesh):
    placed = (
        P(("narrow", "wide"), None),
        P(("narrow", "wide"), None),
        P(("narrow", "wide")),
        P(),
        P(),
        P(),
    )
    return jax.shard_map(
        on_device,
        mesh=mesh,
        in_specs=placed,
        out_specs=(P(("narrow", "wide"), None), P(("narrow", "wide"), None)),
        check_vma=False,
    )
```
